512 devices in a mesh: freq: 32 (over z_lo, y), stn: 16 (over x, z_hi, core).
Axes of the slice: x: 4, y: 4, z: 16 (z_hi: 2, z_lo: 8; z = z_hi * 8 + z_lo), core: 2. Of those that a mesh axis runs over, the one named last changes fastest.
Arguments:
- voltages: bfloat16 [2, 1024, 524288], P(None, 'stn', 'freq'), may hold values from -6 to 6
Outputs:
- visibilities: float32 [32, 2, 1024, 1024], P('freq', None, 'stn')
The draws below stay inside these ranges and needn't reach their ends.
All inputs are finite; a program needn't handle non-finite values.
Results may differ from the reference program's by a relative error of at most 0.0049.
Values may be sent and summed in bfloat16 or wider, within the bound.
No kernel may reach another device: no remote copies, remote signals or barrier semaphores. Data moves between devices by JAX's collectives and lax.ppermute only.
A program may use at most 128 MiB of HBM per device.

```python
import jax
import jax.numpy as jnp
from jax import lax

F = 4096
TAPS = 16
IN_STN = 64
INPUTS = 1024
NB = 128
NS = 113
KEEP = 32
OFFSET = 2032


def block_levels(key, shape, cuts, low, largest):
    loudness, own = 1.0, jax.random.fold_in(key, 6)
    for axis_at, blocks in cuts:
        heights = jnp.exp(jax.random.uniform(jax.random.fold_in(own, axis_at), (blocks,), jnp.float32, low / len(cuts), largest / len(cuts)))
        loudness = loudness * jnp.repeat(heights, shape[axis_at] // blocks).reshape([-1 if axis == axis_at else 1 for axis in range(len(shape))])
    return loudness


def centred(own_key, dims, scale, most, cuts=(), held_as=jnp.bfloat16):
    loudness = block_levels(own_key, dims, cuts, -0.22, 0.18) if cuts else 1.0
    values = jax.random.normal(own_key, dims, jnp.float32) * scale * loudness
    return jnp.minimum(jnp.maximum(values, -most), most).astype(held_as)


def setup_inputs(seed: int = 0) -> dict:
    keys = jax.random.split(jax.random.key(seed), 2)
    voltages = centred(keys[0], (2, INPUTS, NB * F), 1.0, 6.0, ((1, 16), (2, 32)))
    return {"voltages": voltages}


def make_taps(taps_count, points):
    j = jnp.arange(taps_count * points).astype(jnp.float32)
    total = float(taps_count * points)
    proto = jnp.sinc((j - total / 2.0 + 0.5) / points) * (0.5 - 0.5 * jnp.cos(2.0 * jnp.pi * (j + 0.5) / total))
    proto = proto.reshape(taps_count, points)
    return proto / jnp.sqrt(lax.optimization_barrier(jnp.sum(proto * proto, axis=0, keepdims=True)))

def make_table(points, first, count):
    index = jnp.arange(points).astype(jnp.int32)
    chans = (first + jnp.arange(count)).astype(jnp.int32)
    turns = (index[:, None] * chans[None, :] % points).astype(jnp.float32)
    phase = 2.0 * jnp.pi * turns / points
    scale = points ** (-0.5)
    cosine = jnp.cos(phase) * scale
    sine = jnp.sin(phase) * scale
    upper = jnp.stack([cosine, -sine], axis=2).reshape(points, 2 * count)
    lower = jnp.stack([sine, cosine], axis=2).reshape(points, 2 * count)
    return jnp.concatenate([upper, lower], axis=0).astype(jnp.bfloat16)

def channelize(block, taps, table, spectra_count):
    parts, inputs_here, length = block.shape
    points = taps.shape[1]
    samples = block.astype(jnp.float32).reshape(parts, inputs_here, length // points, points)
    filtered = taps[0] * samples[:, :, 0:spectra_count, :]
    for k in range(1, taps.shape[0]):
        filtered = filtered + taps[k] * samples[:, :, k:k + spectra_count, :]
    rows = jnp.transpose(filtered, (2, 1, 0, 3)).reshape(spectra_count * inputs_here, 2 * points)
    spectra = jnp.dot(rows, table.astype(jnp.float32), precision=lax.Precision.HIGHEST, preferred_element_type=jnp.float32).astype(jnp.bfloat16)
    count = table.shape[1] // 2
    spectra = spectra.reshape(spectra_count, inputs_here, count, 2)
    return jnp.transpose(spectra, (2, 3, 0, 1))

def cross_products(left, right, spectra_count):
    full = jnp.einsum('crti,cstj->crsij', left, right, preferred_element_type=jnp.float32)
    real_part = full[:, 0, 0] + full[:, 1, 1]
    imag_part = full[:, 1, 0] - full[:, 0, 1]
    return jnp.stack([real_part, imag_part], axis=1) * (1.0 / spectra_count)

def reference(voltages):
    taps = make_taps(TAPS, F)
    table = make_table(F, OFFSET, KEEP)
    groups = voltages.reshape(2, INPUTS // IN_STN, IN_STN, NB * F)
    groups = jnp.transpose(groups, (1, 0, 2, 3))
    pieces = lax.map(lambda block: channelize(block, taps, table, NS), groups)
    spectra = jnp.transpose(pieces, (1, 2, 3, 0, 4)).reshape(KEEP, 2, NS, INPUTS)

    def one_channel(chan):
        left = chan.astype(jnp.float32)[None]
        return cross_products(left, left, NS)[0]
    return lax.map(one_channel, spectra)
```

```python
import functools

import jax
import jax.numpy as jnp
import numpy as np
from jax import lax
from jax.experimental import pallas as pl
from jax.experimental.pallas import tpu as pltpu
from jax.sharding import PartitionSpec as P

F = 4096
TAPS = 16
NS = 113
KEEP = 32
OFFSET = 2032
BLOCKS = 4
PART = 24
CHUNK = 512
FINE = (7, 8)


def make_taps():
    j = np.arange(TAPS * F, dtype=np.float64)
    total = float(TAPS * F)
    proto = np.sinc((j - total / 2.0 + 0.5) / F) * (
        0.5 - 0.5 * np.cos(2.0 * np.pi * (j + 0.5) / total)
    )
    proto = proto.reshape(TAPS, F)
    return (proto / np.sqrt(np.sum(proto * proto, axis=0, keepdims=True))).astype(np.float32)


def make_table():
    turns = (OFFSET + np.arange(KEEP))[:, None] * np.arange(F)[None, :] % F
    phase = 2.0 * np.pi * turns / F
    both = np.concatenate([np.cos(phase), np.sin(phase)], axis=0) * F**-0.5
    return both.astype(np.float32).astype(jnp.bfloat16)


def channelize_kernel(x0, x1, x2, x3, taps_ref, table_ref, out_ref, acc, parts):
    step = pl.program_id(0)
    table = table_ref[...].astype(jnp.float32)
    coarse, fine = [], []
    for k in range(TAPS):
        weight = table * taps_ref[k : k + 1, :]
        high = weight.astype(jnp.bfloat16)
        coarse.append(high)
        if k in FINE:
            fine.append((weight - high.astype(jnp.float32)).astype(jnp.bfloat16))
    weights = jnp.concatenate(coarse + fine, axis=0)
    samples = jnp.concatenate([x0[...], x1[...], x2[...], x3[...]], axis=0)
    product = lax.dot_general(
        weights, samples, (((1,), (1,)), ((), ())), preferred_element_type=jnp.float32
    )

    @pl.when(step == 0)
    def _():
        acc[...] = product

    @pl.when(step > 0)
    def _():
        acc[...] += product

    @pl.when(step == pl.num_programs(0) - 1)
    def _():
        lane = lax.broadcasted_iota(jnp.int32, (KEEP, 128), 1)
        sign = jnp.where(lane < 64, 1.0, -1.0).astype(jnp.float32)
        for m in range(BLOCKS + TAPS - 1):
            cosine = jnp.zeros((KEEP, 128), jnp.float32)
            sine = jnp.zeros((KEEP, 128), jnp.float32)
            for b in range(BLOCKS):
                k = b + TAPS - 1 - m
                if not 0 <= k < TAPS:
                    continue
                rows = [2 * KEEP * k]
                if k in FINE:
                    rows.append(2 * KEEP * (TAPS + FINE.index(k)))
                for row in rows:
                    cosine += acc[row : row + KEEP, 128 * b : 128 * (b + 1)]
                    sine += acc[row + KEEP : row + 2 * KEEP, 128 * b : 128 * (b + 1)]
            parts[m] = cosine + sign * pltpu.roll(sine, 64, 1)
        for m in range(BLOCKS + TAPS - 1, PART):
            parts[m] = jnp.zeros((KEEP, 128), jnp.float32)
        out_ref[...] = jnp.swapaxes(parts[...], 0, 1).astype(jnp.bfloat16)


def channelize(voltages, taps, table):
    samples = voltages.reshape(128, BLOCKS * F)
    steps = F // CHUNK
    block = lambda b: pl.BlockSpec((128, CHUNK), lambda j, b=b: (0, b * steps + j))
    return pl.pallas_call(
        channelize_kernel,
        grid=(steps,),
        in_specs=[block(b) for b in range(BLOCKS)]
        + [
            pl.BlockSpec((TAPS, CHUNK), lambda j: (0, j)),
            pl.BlockSpec((2 * KEEP, CHUNK), lambda j: (0, j)),
        ],
        out_specs=pl.BlockSpec((KEEP, PART, 128), lambda j: (0, 0, 0)),
        out_shape=jax.ShapeDtypeStruct((KEEP, PART, 128), jnp.bfloat16),
        scratch_shapes=[
            pltpu.VMEM((2 * KEEP * (TAPS + len(FINE)), BLOCKS * 128), jnp.float32),
            pltpu.VMEM((PART, KEEP, 128), jnp.float32),
        ],
        compiler_params=pltpu.CompilerParams(
            dimension_semantics=("arbitrary",), vmem_limit_bytes=40 * 1024 * 1024
        ),
        name="channelize",
    )(samples, samples, samples, samples, taps, table)


def overlap_kernel(recv_ref, out_ref, wide):
    wide[...] = recv_ref[...].astype(jnp.float32).reshape(KEEP * PART, 128)
    block = lax.broadcasted_iota(jnp.int32, (KEEP, 128), 0)
    for r in range(BLOCKS):
        total = jnp.zeros((KEEP, 128), jnp.float32)
        for a in range((TAPS - 1 + BLOCKS - 1) // BLOCKS + 1):
            m = BLOCKS * a + r
            if m >= BLOCKS + TAPS - 1:
                continue
            share = wide[pl.ds(m, KEEP, stride=PART), :]
            if a:
                share = jnp.where(block >= a, pltpu.roll(share, a, 0), 0.0)
            total += share
        total = jnp.where(BLOCKS * block + r >= TAPS - 1, total, 0.0)
        out_ref[KEEP * r : KEEP * (r + 1), :] = total.astype(jnp.bfloat16)


def overlap(recv):
    return pl.pallas_call(
        overlap_kernel,
        out_shape=jax.ShapeDtypeStruct((BLOCKS * KEEP, 128), jnp.bfloat16),
        scratch_shapes=[pltpu.VMEM((KEEP * PART, 128), jnp.float32)],
        name="overlap",
    )(recv)


def products_kernel(mine_ref, all_ref, out_ref):
    mine = mine_ref[...].astype(jnp.float32)
    lane = lax.broadcasted_iota(jnp.int32, mine.shape, 1)
    turned = pltpu.roll(mine, 64, 1) * jnp.where(lane < 64, 1.0, -1.0)
    left = jnp.concatenate([mine, turned], axis=0).astype(jnp.bfloat16)
    first = lane < 64
    for pair in range(all_ref.shape[0] // 2):
        one = all_ref[2 * pair].astype(jnp.float32)
        two = all_ref[2 * pair + 1].astype(jnp.float32)
        real = jnp.where(first, one, pltpu.roll(two, 64, 1))
        imag = jnp.where(first, pltpu.roll(one, 64, 1), two)
        right = jnp.concatenate([real, imag], axis=0).astype(jnp.bfloat16)
        full = lax.dot_general(
            left, right, (((0,), (0,)), ((), ())), preferred_element_type=jnp.float32
        ) * (1.0 / NS)
        out_ref[0, 0, :, 128 * pair : 128 * (pair + 1)] = full[:64]
        out_ref[0, 1, :, 128 * pair : 128 * (pair + 1)] = full[64:]


def products(mine, everyone):
    return pl.pallas_call(
        products_kernel,
        out_shape=jax.ShapeDtypeStruct((1, 2, 64, 64 * everyone.shape[0]), jnp.float32),
        name="products",
    )(mine, everyone)


def body(voltages):
    taps = jnp.asarray(make_taps())
    table = jnp.asarray(make_table())
    sent = channelize(voltages, taps, table)
    recv = lax.all_to_all(sent, "freq", split_axis=0, concat_axis=0, tiled=True)
    mine = overlap(recv)
    everyone = lax.all_gather(mine, "stn", axis=0)
    return products(mine, everyone)


def solution(mesh):
    return jax.shard_map(
        body,
        mesh=mesh,
        in_specs=(P(None, "stn", "freq"),),
        out_specs=P("freq", None, "stn", None),
        check_vma=False,
    )
```

```python
import jax
import jax.numpy as jnp
import numpy as np
from jax import lax
from jax.experimental import pallas as pl
from jax.experimental.pallas import tpu as pltpu
from jax.sharding import Mesh
from jax.sharding import PartitionSpec as P

F = 4096
TAPS = 16
NS = 113
KEEP = 32
HALF = KEEP // 2
MIDDLE = F // 2
BLOCKS = 4
GROUPS = 5
CHUNK = 1024
STEPS = F // CHUNK
FINE = (7, 8)
EDGE = KEEP * TAPS
FINES = EDGE + KEEP
FINE_EDGE = FINES + KEEP * len(FINE)
ROWS = FINE_EDGE + KEEP


def make_taps():
    j = np.arange(TAPS * F, dtype=np.float64)
    total = float(TAPS * F)
    proto = np.sinc((j - total / 2.0 + 0.5) / F) * (
        0.5 - 0.5 * np.cos(2.0 * np.pi * (j + 0.5) / total)
    )
    proto = proto.reshape(TAPS, F)
    taps = proto / np.sqrt(np.sum(proto * proto, axis=0, keepdims=True))
    return taps[::-1].astype(np.float32)


def make_table():
    turns = (MIDDLE + np.arange(HALF + 1))[:, None] * np.arange(F)[None, :] % F
    phase = 2.0 * np.pi * turns / F
    cosine, sine = np.cos(phase) * F**-0.5, np.sin(phase) * F**-0.5
    rows = [cosine[:HALF], sine[:HALF], cosine[HALF:], sine[HALF:], np.zeros((6, F))]
    table = np.concatenate(rows, axis=0).astype(np.float32)
    return table.astype(jnp.bfloat16).astype(np.float32)


def split(weight):
    high = weight.astype(jnp.bfloat16)
    return high, (weight - high.astype(jnp.float32)).astype(jnp.bfloat16)


def channelize_kernel(x_hbm, taps_hbm, table_hbm, out_ref, x, taps, table, acc, parts, sems):
    first = [
        pltpu.make_async_copy(taps_hbm, taps, sems.at[0]),
        pltpu.make_async_copy(table_hbm, table, sems.at[1]),
    ]
    for copy in first:
        copy.start()
    copies = []
    for j in range(STEPS):
        for b in range(BLOCKS):
            at = pl.ds(b * F + j * CHUNK, CHUNK)
            copy = pltpu.make_async_copy(
                x_hbm.at[:, at], x.at[:, at], sems.at[2 + j * BLOCKS + b]
            )
            copy.start()
            copies.append(copy)
    for copy in first:
        copy.wait()

    for j in range(STEPS):
        here = slice(j * CHUNK, (j + 1) * CHUNK)
        tap = taps[:, here]
        wide = table[:, here]
        main, fine = [], []
        for i in range(TAPS):
            high, low = split(wide[:KEEP] * tap[i : i + 1])
            main.append(high)
            if i in FINE:
                fine.append(low)
        edge = jnp.concatenate([tap * wide[KEEP : KEEP + 1], tap * wide[KEEP + 1 : KEEP + 2]], axis=0)
        high, low = split(edge)
        weights = jnp.concatenate(main + [high] + fine + [low], axis=0)
        for copy in copies[j * BLOCKS : (j + 1) * BLOCKS]:
            copy.wait()
        samples = jnp.concatenate(
            [x[:, b * F + j * CHUNK : b * F + (j + 1) * CHUNK] for b in range(BLOCKS)], axis=0
        )
        product = lax.dot_general(
            weights, samples, (((1,), (1,)), ((), ())), preferred_element_type=jnp.float32
        )
        if j == 0:
            acc[...] = product
        else:
            acc[...] += product

    lane = lax.broadcasted_iota(jnp.int32, (1, 128), 1)
    sign = jnp.where(lane < 64, 1.0, -1.0).astype(jnp.float32)
    for m in range(GROUPS * BLOCKS):
        cosine = jnp.zeros((HALF, 128), jnp.float32)
        sine = jnp.zeros((HALF, 128), jnp.float32)
        for b in range(BLOCKS):
            i = m - b
            if not 0 <= i < TAPS:
                continue
            rows = [KEEP * i]
            if i in FINE:
                rows.append(FINES + KEEP * FINE.index(i))
            for row in rows:
                cosine += acc[row : row + HALF, 128 * b : 128 * (b + 1)]
                sine += acc[row + HALF : row + KEEP, 128 * b : 128 * (b + 1)]
        turned = sign * pltpu.roll(sine, 64, 1)
        parts[KEEP * m : KEEP * m + HALF, :] = cosine + turned
        parts[KEEP * m + HALF : KEEP * (m + 1), :] = cosine - turned

    def put(channel, group, rows):
        rows = rows.astype(jnp.bfloat16)
        out_ref[channel, group] = rows
        out_ref[KEEP + channel, group] = rows

    for p in range(HALF):
        for a in range(GROUPS):
            above = parts[pl.ds(KEEP * BLOCKS * a + p, BLOCKS, stride=KEEP), :]
            put(HALF + p, a, above)
            if p:
                below = parts[pl.ds(KEEP * BLOCKS * a + HALF + p, BLOCKS, stride=KEEP), :]
                put(HALF - p, a, below)
    edge = acc[EDGE:FINES, :] + acc[FINE_EDGE:ROWS, :]
    total = jnp.zeros((GROUPS * BLOCKS, 128), jnp.float32)
    for b in range(BLOCKS):
        cosine = edge[:TAPS, 128 * b : 128 * (b + 1)]
        sine = edge[TAPS:, 128 * b : 128 * (b + 1)]
        share = cosine - sign * pltpu.roll(sine, 64, 1)
        pieces = [share]
        if b:
            pieces.insert(0, jnp.zeros((b, 128), jnp.float32))
        if b < BLOCKS:
            pieces.append(jnp.zeros((BLOCKS - b, 128), jnp.float32))
        total += jnp.concatenate(pieces, axis=0)
    for a in range(GROUPS):
        put(0, a, total[BLOCKS * a : BLOCKS * (a + 1)])


def channelize(voltages, taps, table):
    samples = voltages.reshape(128, BLOCKS * F)
    samples, taps, table = (
        pltpu.with_memory_space_constraint(array, pltpu.HBM) for array in (samples, taps, table)
    )
    anywhere = pl.BlockSpec(memory_space=pltpu.HBM)
    return pl.pallas_call(
        channelize_kernel,
        in_specs=[anywhere] * 3,
        out_shape=jax.ShapeDtypeStruct((2 * KEEP, GROUPS, BLOCKS, 128), jnp.bfloat16),
        scratch_shapes=[
            pltpu.VMEM((128, BLOCKS * F), jnp.bfloat16),
            pltpu.VMEM((TAPS, F), jnp.float32),
            pltpu.VMEM((40, F), jnp.float32),
            pltpu.VMEM((ROWS, BLOCKS * 128), jnp.float32),
            pltpu.VMEM((GROUPS * BLOCKS * KEEP, 128), jnp.float32),
            pltpu.SemaphoreType.DMA((2 + STEPS * BLOCKS,)),
        ],
        compiler_params=pltpu.CompilerParams(vmem_limit_bytes=40 * 1024 * 1024),
        name="channelize",
    )(samples, taps, table)


def overlap_kernel(recv_ref, out_ref, wide):
    row = lax.broadcasted_iota(jnp.int32, (BLOCKS, 128), 0)
    for z in range(2):
        for d in range(KEEP):
            total = jnp.zeros((BLOCKS, 128), jnp.float32)
            if BLOCKS * (d + 1) >= TAPS:
                for a in range(min(d + 1, GROUPS)):
                    total += recv_ref[KEEP * z + d - a, a].astype(jnp.float32)
                if BLOCKS * d < TAPS - 1:
                    total = jnp.where(BLOCKS * d + row >= TAPS - 1, total, 0.0)
            at = KEEP * BLOCKS * z + BLOCKS * d
            wide[at : at + BLOCKS, :] = total
    done = wide[...].astype(jnp.bfloat16).reshape(2, BLOCKS * KEEP, 128)
    for x in range(out_ref.shape[0]):
        out_ref[x] = done


def overlap(recv, copies):
    return pl.pallas_call(
        overlap_kernel,
        out_shape=jax.ShapeDtypeStruct((copies, 2, BLOCKS * KEEP, 128), jnp.bfloat16),
        scratch_shapes=[pltpu.VMEM((2 * BLOCKS * KEEP, 128), jnp.float32)],
        name="overlap",
    )(recv)


def products_kernel(me_ref, all_ref, out_ref):
    mine = all_ref[me_ref[0], me_ref[1]].astype(jnp.float32)
    lane = lax.broadcasted_iota(jnp.int32, mine.shape, 1)
    turned = pltpu.roll(mine, 64, 1) * jnp.where(lane < 64, 1.0, -1.0)
    left = jnp.concatenate([mine, turned], axis=0).astype(jnp.bfloat16)
    first = lane < 64
    for pair in range(all_ref.shape[1]):
        one = all_ref[0, pair].astype(jnp.float32)
        two = all_ref[1, pair].astype(jnp.float32)
        real = jnp.where(first, one, pltpu.roll(two, 64, 1))
        imag = jnp.where(first, pltpu.roll(one, 64, 1), two)
        right = jnp.concatenate([real, imag], axis=0).astype(jnp.bfloat16)
        full = lax.dot_general(
            left, right, (((0,), (0,)), ((), ())), preferred_element_type=jnp.float32
        ) * (1.0 / NS)
        out_ref[0, 0, :, 128 * pair : 128 * (pair + 1)] = full[:64]
        out_ref[0, 1, :, 128 * pair : 128 * (pair + 1)] = full[64:]


def products(me, everyone):
    pairs = everyone.shape[1]
    return pl.pallas_call(
        products_kernel,
        in_specs=[
            pl.BlockSpec(memory_space=pltpu.SMEM),
            pl.BlockSpec(memory_space=pltpu.VMEM),
        ],
        out_shape=jax.ShapeDtypeStruct((1, 2, 64, 128 * pairs), jnp.float32),
        name="products",
    )(me, everyone)


def body(voltages):
    taps = jnp.asarray(make_taps())
    table = jnp.asarray(make_table())
    sent = channelize(voltages, taps, table)
    recv = lax.all_to_all(sent, ("zh", "zl", "y"), split_axis=0, concat_axis=0, tiled=True)
    mine = overlap(recv, 4)
    row = lax.all_to_all(mine, "x", split_axis=0, concat_axis=0, tiled=True)
    row = row.reshape(8, BLOCKS * KEEP, 128)
    everyone = lax.all_gather(row, "c", axis=0)
    me = jnp.stack([lax.axis_index("c"), 2 * lax.axis_index("x") + lax.axis_index("zh")])
    return products(me.astype(jnp.int32), everyone)


def solution(mesh):
    fine = Mesh(mesh.devices.reshape(8, 4, 4, 2, 2), ("zl", "y", "x", "zh", "c"))
    return jax.shard_map(
        body,
        mesh=fine,
        in_specs=(P(None, ("x", "zh", "c"), ("zl", "y")),),
        out_specs=P(("zl", "y"), None, ("x", "zh", "c"), None),
        check_vma=False,
    )
```

```python
import jax
import jax.numpy as jnp
import numpy as np
from jax import lax
from jax.experimental import pallas as pl
from jax.experimental.pallas import tpu as pltpu
from jax.sharding import Mesh
from jax.sharding import PartitionSpec as P

F = 4096
TAPS = 16
NS = 113
KEEP = 32
HALF = KEEP // 2
MIDDLE = F // 2
BLOCKS = 4
GROUPS = 5
ROW = 4
LINE = KEEP // ROW
SPAN = 32
CUTS = (0, 512, 1536, 2816, 4096)
STEPS = len(CUTS) - 1
FINE = (7, 8)
EDGE = KEEP * TAPS
FINES = EDGE + KEEP
FINE_EDGE = FINES + KEEP * len(FINE)
ROWS = FINE_EDGE + KEEP


def make_taps():
    j = np.arange(TAPS * F, dtype=np.float64)
    total = float(TAPS * F)
    proto = np.sinc((j - total / 2.0 + 0.5) / F) * (
        0.5 - 0.5 * np.cos(2.0 * np.pi * (j + 0.5) / total)
    )
    proto = proto.reshape(TAPS, F)
    taps = proto / np.sqrt(np.sum(proto * proto, axis=0, keepdims=True))
    return taps[::-1].astype(np.float32)


def make_table():
    turns = (MIDDLE + np.arange(HALF + 1))[:, None] * np.arange(F)[None, :] % F
    phase = 2.0 * np.pi * turns / F
    cosine, sine = np.cos(phase) * F**-0.5, np.sin(phase) * F**-0.5
    rows = [cosine[:HALF], sine[:HALF], cosine[HALF:], sine[HALF:], np.zeros((6, F))]
    table = np.concatenate(rows, axis=0).astype(np.float32)
    return table.astype(jnp.bfloat16).astype(np.float32)


def split(weight):
    high = weight.astype(jnp.bfloat16)
    return high, (weight - high.astype(jnp.float32)).astype(jnp.bfloat16)


def channelize_kernel(x_hbm, taps_hbm, table_hbm, out_ref, x, taps, table, acc, parts, sems):
    copies = []
    for j in range(STEPS):
        size = CUTS[j + 1] - CUTS[j]
        here = pl.ds(CUTS[j], size)
        own = [
            pltpu.make_async_copy(taps_hbm.at[:, here], taps.at[:, here], sems.at[j, 0]),
            pltpu.make_async_copy(table_hbm.at[:, here], table.at[:, here], sems.at[j, 1]),
        ]
        for b in range(BLOCKS):
            at = pl.ds(b * F + CUTS[j], size)
            own.append(pltpu.make_async_copy(x_hbm.at[:, at], x.at[:, at], sems.at[j, 2 + b]))
        for copy in own:
            copy.start()
        copies.append(own)

    for j in range(STEPS):
        here = slice(CUTS[j], CUTS[j + 1])
        for copy in copies[j][:2]:
            copy.wait()
        tap = taps[:, here]
        wide = table[:, here]
        main, fine = [], []
        for i in range(TAPS):
            high, low = split(wide[:KEEP] * tap[i : i + 1])
            main.append(high)
            if i in FINE:
                fine.append(low)
        edge = jnp.concatenate([tap * wide[KEEP : KEEP + 1], tap * wide[KEEP + 1 : KEEP + 2]], axis=0)
        high, low = split(edge)
        weights = jnp.concatenate(main + [high] + fine + [low], axis=0)
        for copy in copies[j][2:]:
            copy.wait()
        samples = jnp.concatenate(
            [x[:, b * F + CUTS[j] : b * F + CUTS[j + 1]] for b in range(BLOCKS)], axis=0
        )
        product = lax.dot_general(
            weights, samples, (((1,), (1,)), ((), ())), preferred_element_type=jnp.float32
        )
        if j == 0:
            acc[...] = product
        else:
            acc[...] += product

    lane = lax.broadcasted_iota(jnp.int32, (1, 128), 1)
    sign = jnp.where(lane < 64, 1.0, -1.0).astype(jnp.float32)
    for m in range(GROUPS * BLOCKS):
        cosine = jnp.zeros((HALF, 128), jnp.float32)
        sine = jnp.zeros((HALF, 128), jnp.float32)
        for b in range(BLOCKS):
            i = m - b
            if not 0 <= i < TAPS:
                continue
            rows = [KEEP * i]
            if i in FINE:
                rows.append(FINES + KEEP * FINE.index(i))
            for row in rows:
                cosine += acc[row : row + HALF, 128 * b : 128 * (b + 1)]
                sine += acc[row + HALF : row + KEEP, 128 * b : 128 * (b + 1)]
        turned = sign * pltpu.roll(sine, 64, 1)
        parts[KEEP * m : KEEP * m + HALF, :] = cosine + turned
        parts[KEEP * m + HALF : KEEP * (m + 1), :] = cosine - turned

    def put(channel, group, rows):
        out_ref[channel % ROW, channel // ROW, group] = rows

    for p in range(HALF):
        for a in range(GROUPS):
            above = parts[pl.ds(KEEP * BLOCKS * a + p, BLOCKS, stride=KEEP), :]
            put(HALF + p, a, above)
            if p:
                below = parts[pl.ds(KEEP * BLOCKS * a + HALF + p, BLOCKS, stride=KEEP), :]
                put(HALF - p, a, below)
    edge = acc[EDGE:FINES, :] + acc[FINE_EDGE:ROWS, :]
    total = jnp.zeros((GROUPS * BLOCKS, 128), jnp.float32)
    for b in range(BLOCKS):
        cosine = edge[:TAPS, 128 * b : 128 * (b + 1)]
        sine = edge[TAPS:, 128 * b : 128 * (b + 1)]
        share = cosine - sign * pltpu.roll(sine, 64, 1)
        pieces = [share]
        if b:
            pieces.insert(0, jnp.zeros((b, 128), jnp.float32))
        if b < BLOCKS:
            pieces.append(jnp.zeros((BLOCKS - b, 128), jnp.float32))
        total += jnp.concatenate(pieces, axis=0)
    for a in range(GROUPS):
        put(0, a, total[BLOCKS * a : BLOCKS * (a + 1)])


def channelize(voltages, taps, table):
    samples = voltages.reshape(128, BLOCKS * F)
    samples, taps, table = (
        pltpu.with_memory_space_constraint(array, pltpu.HBM) for array in (samples, taps, table)
    )
    anywhere = pl.BlockSpec(memory_space=pltpu.HBM)
    return pl.pallas_call(
        channelize_kernel,
        in_specs=[anywhere] * 3,
        out_shape=jax.ShapeDtypeStruct((ROW, LINE, GROUPS, BLOCKS, 128), jnp.float32),
        scratch_shapes=[
            pltpu.VMEM((128, BLOCKS * F), jnp.bfloat16),
            pltpu.VMEM((TAPS, F), jnp.float32),
            pltpu.VMEM((40, F), jnp.float32),
            pltpu.VMEM((ROWS, BLOCKS * 128), jnp.float32),
            pltpu.VMEM((GROUPS * BLOCKS * KEEP, 128), jnp.float32),
            pltpu.SemaphoreType.DMA((STEPS, 2 + BLOCKS)),
        ],
        compiler_params=pltpu.CompilerParams(vmem_limit_bytes=40 * 1024 * 1024),
        name="channelize",
    )(samples, taps, table)


def row_kernel(recv_ref, out_ref, wide):
    for g in range(SPAN // BLOCKS):
        total = None
        for y in range(ROW):
            if 0 <= g - y < GROUPS:
                share = recv_ref[y, :, g - y]
                total = share if total is None else total + share
        wide[:, BLOCKS * g : BLOCKS * (g + 1), :] = total
    done = wide[...].astype(jnp.bfloat16)
    out_ref[:LINE] = done
    out_ref[LINE:] = done


def add_row(recv):
    recv = pltpu.with_memory_space_constraint(recv, pltpu.VMEM)
    return pl.pallas_call(
        row_kernel,
        in_specs=[pl.BlockSpec(memory_space=pltpu.VMEM)],
        out_specs=pl.BlockSpec(memory_space=pltpu.VMEM),
        out_shape=pltpu.VMEM((2 * LINE, SPAN, 128), jnp.bfloat16),
        scratch_shapes=[pltpu.VMEM((LINE, SPAN, 128), jnp.float32)],
        name="add_row",
    )(recv)


def line_kernel(recv_ref, out_ref):
    for z in range(2):
        for d in range(LINE):
            total = recv_ref[LINE * z + d, :TAPS].astype(jnp.float32)
            if d:
                total += recv_ref[LINE * z + d - 1, TAPS:].astype(jnp.float32)
            else:
                row = lax.broadcasted_iota(jnp.int32, total.shape, 0)
                total = jnp.where(row == TAPS - 1, total, 0.0)
            done = total.astype(jnp.bfloat16)
            for x in range(out_ref.shape[0]):
                out_ref[x, z, TAPS * d : TAPS * (d + 1), :] = done


def add_line(recv, copies):
    recv = pltpu.with_memory_space_constraint(recv, pltpu.VMEM)
    return pl.pallas_call(
        line_kernel,
        in_specs=[pl.BlockSpec(memory_space=pltpu.VMEM)],
        out_specs=pl.BlockSpec(memory_space=pltpu.VMEM),
        out_shape=pltpu.VMEM((copies, 2, BLOCKS * KEEP, 128), jnp.bfloat16),
        name="add_line",
    )(recv)


def products_kernel(all_ref, out_hbm, done, sems):
    own = 2 * lax.axis_index("x") + lax.axis_index("zh")
    mine = all_ref[lax.axis_index("c"), own].astype(jnp.float32)
    lane = lax.broadcasted_iota(jnp.int32, mine.shape, 1)
    first = lane < 64
    turned = pltpu.roll(mine, 64, 1) * jnp.where(first, 1.0, -1.0)
    left = jnp.concatenate([mine.T, turned.T], axis=1).astype(jnp.bfloat16)
    copies = []
    for x in range(all_ref.shape[1] // 2):
        real, imag = [], []
        for pair in (2 * x, 2 * x + 1):
            one = all_ref[0, pair].astype(jnp.float32)
            two = all_ref[1, pair].astype(jnp.float32)
            real.append(jnp.where(first, one, pltpu.roll(two, 64, 1)))
            imag.append(jnp.where(first, pltpu.roll(one, 64, 1), two))
        right = jnp.concatenate(
            [jnp.concatenate(real, axis=1), jnp.concatenate(imag, axis=1)], axis=0
        ).astype(jnp.bfloat16)
        full = jnp.dot(left, right, preferred_element_type=jnp.float32) * (1.0 / NS)
        here = slice(256 * x, 256 * (x + 1))
        done[0, :, here] = full[:64]
        done[1, :, here] = full[64:]
        at = pl.ds(256 * x, 256)
        copy = pltpu.make_async_copy(done.at[:, :, at], out_hbm.at[0, :, :, at], sems.at[x])
        copy.start()
        copies.append(copy)
    for copy in copies:
        copy.wait()


def products(everyone):
    inputs = 128 * everyone.shape[1]
    everyone = pltpu.with_memory_space_constraint(everyone, pltpu.VMEM)
    return pl.pallas_call(
        products_kernel,
        in_specs=[pl.BlockSpec(memory_space=pltpu.VMEM)],
        out_specs=pl.BlockSpec(memory_space=pltpu.HBM),
        out_shape=jax.ShapeDtypeStruct((1, 2, 64, inputs), jnp.float32),
        scratch_shapes=[
            pltpu.VMEM((2, 64, inputs), jnp.float32),
            pltpu.SemaphoreType.DMA((inputs // 256,)),
        ],
        name="products",
    )(everyone)


def body(voltages):
    taps = jnp.asarray(make_taps())
    table = jnp.asarray(make_table())
    sent = channelize(voltages, taps, table)
    recv = lax.all_to_all(sent, "y", split_axis=0, concat_axis=0, tiled=True)
    line = add_row(recv)
    recv = lax.all_to_all(line, ("zh", "zl"), split_axis=0, concat_axis=0, tiled=True)
    mine = add_line(recv, 4)
    row = lax.all_to_all(mine, "x", split_axis=0, concat_axis=0, tiled=True)
    row = row.reshape(8, BLOCKS * KEEP, 128)
    everyone = lax.all_gather(row, "c", axis=0)
    return products(everyone)


def solution(mesh):
    fine = Mesh(mesh.devices.reshape(8, 4, 4, 2, 2), ("zl", "y", "x", "zh", "c"))
    return jax.shard_map(
        body,
        mesh=fine,
        in_specs=(P(None, ("x", "zh", "c"), ("zl", "y")),),
        out_specs=P(("zl", "y"), None, ("x", "zh", "c"), None),
        check_vma=False,
    )
```

```python
import jax
import jax.numpy as jnp
import numpy as np
from jax import lax
from jax.experimental import pallas as pl
from jax.experimental.pallas import tpu as pltpu
from jax.sharding import Mesh
from jax.sharding import PartitionSpec as P

F = 4096
TAPS = 16
NS = 113
KEEP = 32
HALF = KEEP // 2
MIDDLE = F // 2
BLOCKS = 4
GROUPS = 5
ROW = 4
LINE = KEEP // ROW
SPAN = 32
CUTS = (0, 1024, 2560, 4096)
STEPS = len(CUTS) - 1
FINE = (7, 8)
EDGE = KEEP * TAPS
FINES = EDGE + KEEP
FINE_EDGE = FINES + KEEP * len(FINE)
ROWS = FINE_EDGE + KEEP


def make_taps():
    j = np.arange(TAPS * F, dtype=np.float64)
    total = float(TAPS * F)
    proto = np.sinc((j - total / 2.0 + 0.5) / F) * (
        0.5 - 0.5 * np.cos(2.0 * np.pi * (j + 0.5) / total)
    )
    proto = proto.reshape(TAPS, F)
    taps = proto / np.sqrt(np.sum(proto * proto, axis=0, keepdims=True))
    return taps[::-1].astype(np.float32)


def make_table():
    turns = (MIDDLE + np.arange(HALF + 1))[:, None] * np.arange(F)[None, :] % F
    phase = 2.0 * np.pi * turns / F
    cosine, sine = np.cos(phase) * F**-0.5, np.sin(phase) * F**-0.5
    rows = [cosine[:HALF], sine[:HALF], cosine[HALF:], sine[HALF:], np.zeros((6, F))]
    table = np.concatenate(rows, axis=0).astype(np.float32)
    return table.astype(jnp.bfloat16).astype(np.float32)


def split(weight):
    high = weight.astype(jnp.bfloat16)
    return high, (weight - high.astype(jnp.float32)).astype(jnp.bfloat16)


def channelize_kernel(x_hbm, taps_hbm, table_hbm, out_ref, x, taps, table, acc, parts, sems):
    copies = []
    for j in range(STEPS):
        size = CUTS[j + 1] - CUTS[j]
        here = pl.ds(CUTS[j], size)
        own = [
            pltpu.make_async_copy(taps_hbm.at[:, here], taps.at[:, here], sems.at[j, 0]),
            pltpu.make_async_copy(table_hbm.at[:, here], table.at[:, here], sems.at[j, 1]),
        ]
        for b in range(BLOCKS):
            at = pl.ds(b * F + CUTS[j], size)
            copy = pltpu.make_async_copy(
                x_hbm.at[:, at], x.at[128 * b : 128 * (b + 1), here], sems.at[j, 2 + b]
            )
            own.append(copy)
        for copy in own:
            copy.start()
        copies.append(own)

    for j in range(STEPS):
        here = slice(CUTS[j], CUTS[j + 1])
        for copy in copies[j][:2]:
            copy.wait()
        tap = taps[:, here]
        wide = table[:, here]
        main, fine = [], []
        for i in range(TAPS):
            high, low = split(wide[:KEEP] * tap[i : i + 1])
            main.append(high)
            if i in FINE:
                fine.append(low)
        edge = jnp.concatenate([tap * wide[KEEP : KEEP + 1], tap * wide[KEEP + 1 : KEEP + 2]], axis=0)
        high, low = split(edge)
        weights = jnp.concatenate(main + [high] + fine + [low], axis=0)
        for copy in copies[j][2:]:
            copy.wait()
        product = lax.dot_general(
            weights, x[:, here], (((1,), (1,)), ((), ())), preferred_element_type=jnp.float32
        )
        if j == 0:
            acc[...] = product
        else:
            acc[...] += product

    lane = lax.broadcasted_iota(jnp.int32, (1, 128), 1)
    sign = jnp.where(lane < 64, 1.0, -1.0).astype(jnp.float32)
    for m in range(GROUPS * BLOCKS):
        cosine = jnp.zeros((HALF, 128), jnp.float32)
        sine = jnp.zeros((HALF, 128), jnp.float32)
        for b in range(BLOCKS):
            i = m - b
            if not 0 <= i < TAPS:
                continue
            rows = [KEEP * i]
            if i in FINE:
                rows.append(FINES + KEEP * FINE.index(i))
            for row in rows:
                cosine += acc[row : row + HALF, 128 * b : 128 * (b + 1)]
                sine += acc[row + HALF : row + KEEP, 128 * b : 128 * (b + 1)]
        turned = sign * pltpu.roll(sine, 64, 1)
        parts[KEEP * m : KEEP * m + HALF, :] = cosine + turned
        parts[KEEP * m + HALF : KEEP * (m + 1), :] = cosine - turned

    def put(channel, group, rows):
        out_ref[channel % ROW, channel // ROW, group] = rows.astype(jnp.bfloat16)

    for p in range(HALF):
        for a in range(GROUPS):
            above = parts[pl.ds(KEEP * BLOCKS * a + p, BLOCKS, stride=KEEP), :]
            put(HALF + p, a, above)
            if p:
                below = parts[pl.ds(KEEP * BLOCKS * a + HALF + p, BLOCKS, stride=KEEP), :]
                put(HALF - p, a, below)
    edge = acc[EDGE:FINES, :] + acc[FINE_EDGE:ROWS, :]
    total = jnp.zeros((GROUPS * BLOCKS, 128), jnp.float32)
    for b in range(BLOCKS):
        cosine = edge[:TAPS, 128 * b : 128 * (b + 1)]
        sine = edge[TAPS:, 128 * b : 128 * (b + 1)]
        share = cosine - sign * pltpu.roll(sine, 64, 1)
        pieces = [share]
        if b:
            pieces.insert(0, jnp.zeros((b, 128), jnp.float32))
        if b < BLOCKS:
            pieces.append(jnp.zeros((BLOCKS - b, 128), jnp.float32))
        total += jnp.concatenate(pieces, axis=0)
    for a in range(GROUPS):
        put(0, a, total[BLOCKS * a : BLOCKS * (a + 1)])


def channelize(voltages, taps, table):
    samples = voltages.reshape(128, BLOCKS * F)
    samples, taps, table = (
        pltpu.with_memory_space_constraint(array, pltpu.HBM) for array in (samples, taps, table)
    )
    anywhere = pl.BlockSpec(memory_space=pltpu.HBM)
    return pl.pallas_call(
        channelize_kernel,
        in_specs=[anywhere] * 3,
        out_specs=pl.BlockSpec(memory_space=pltpu.VMEM),
        out_shape=pltpu.VMEM((ROW, LINE, GROUPS, BLOCKS, 128), jnp.bfloat16),
        scratch_shapes=[
            pltpu.VMEM((128 * BLOCKS, F), jnp.bfloat16),
            pltpu.VMEM((TAPS, F), jnp.float32),
            pltpu.VMEM((40, F), jnp.float32),
            pltpu.VMEM((ROWS, BLOCKS * 128), jnp.float32),
            pltpu.VMEM((GROUPS * BLOCKS * KEEP, 128), jnp.float32),
            pltpu.SemaphoreType.DMA((STEPS, 2 + BLOCKS)),
        ],
        compiler_params=pltpu.CompilerParams(vmem_limit_bytes=40 * 1024 * 1024),
        name="channelize",
    )(samples, taps, table)


def row_kernel(recv_ref, out_ref, wide):
    for g in range(SPAN // BLOCKS):
        total = None
        for y in range(ROW):
            if 0 <= g - y < GROUPS:
                share = recv_ref[y, :, g - y].astype(jnp.float32)
                total = share if total is None else total + share
        wide[:, BLOCKS * g : BLOCKS * (g + 1), :] = total
    done = wide[...].astype(jnp.bfloat16)
    out_ref[:LINE] = done
    out_ref[LINE:] = done


def add_row(recv):
    recv = pltpu.with_memory_space_constraint(recv, pltpu.VMEM)
    return pl.pallas_call(
        row_kernel,
        in_specs=[pl.BlockSpec(memory_space=pltpu.VMEM)],
        out_specs=pl.BlockSpec(memory_space=pltpu.VMEM),
        out_shape=pltpu.VMEM((2 * LINE, SPAN, 128), jnp.bfloat16),
        scratch_shapes=[pltpu.VMEM((LINE, SPAN, 128), jnp.float32)],
        name="add_row",
    )(recv)


def line_kernel(recv_ref, out_ref):
    for z in range(2):
        for d in range(LINE):
            total = recv_ref[LINE * z + d, :TAPS].astype(jnp.float32)
            if d:
                total += recv_ref[LINE * z + d - 1, TAPS:].astype(jnp.float32)
            else:
                row = lax.broadcasted_iota(jnp.int32, total.shape, 0)
                total = jnp.where(row == TAPS - 1, total, 0.0)
            done = total.astype(jnp.bfloat16)
            for x in range(out_ref.shape[0]):
                out_ref[x, z, TAPS * d : TAPS * (d + 1), :] = done


def add_line(recv, copies):
    recv = pltpu.with_memory_space_constraint(recv, pltpu.VMEM)
    return pl.pallas_call(
        line_kernel,
        in_specs=[pl.BlockSpec(memory_space=pltpu.VMEM)],
        out_specs=pl.BlockSpec(memory_space=pltpu.VMEM),
        out_shape=pltpu.VMEM((copies, 2, BLOCKS * KEEP, 128), jnp.bfloat16),
        name="add_line",
    )(recv)


def products_kernel(all_ref, out_hbm, done, sems):
    own = 2 * lax.axis_index("x") + lax.axis_index("zh")
    mine = all_ref[lax.axis_index("c"), own].astype(jnp.float32)
    lane = lax.broadcasted_iota(jnp.int32, mine.shape, 1)
    first = lane < 64
    turned = pltpu.roll(mine, 64, 1) * jnp.where(first, 1.0, -1.0)
    left = jnp.concatenate([mine.T, turned.T], axis=1).astype(jnp.bfloat16)
    copies = []
    for x in range(all_ref.shape[1] // 2):
        real, imag = [], []
        for pair in (2 * x, 2 * x + 1):
            one = all_ref[0, pair].astype(jnp.float32)
            two = all_ref[1, pair].astype(jnp.float32)
            real.append(jnp.where(first, one, pltpu.roll(two, 64, 1)))
            imag.append(jnp.where(first, pltpu.roll(one, 64, 1), two))
        right = jnp.concatenate(
            [jnp.concatenate(real, axis=1), jnp.concatenate(imag, axis=1)], axis=0
        ).astype(jnp.bfloat16)
        full = jnp.dot(left, right, preferred_element_type=jnp.float32) * (1.0 / NS)
        here = slice(256 * x, 256 * (x + 1))
        done[0, :, here] = full[:64]
        done[1, :, here] = full[64:]
        at = pl.ds(256 * x, 256)
        copy = pltpu.make_async_copy(done.at[:, :, at], out_hbm.at[0, :, :, at], sems.at[x])
        copy.start()
        copies.append(copy)
    for copy in copies:
        copy.wait()


def products(everyone):
    inputs = 128 * everyone.shape[1]
    everyone = pltpu.with_memory_space_constraint(everyone, pltpu.VMEM)
    return pl.pallas_call(
        products_kernel,
        in_specs=[pl.BlockSpec(memory_space=pltpu.VMEM)],
        out_specs=pl.BlockSpec(memory_space=pltpu.HBM),
        out_shape=jax.ShapeDtypeStruct((1, 2, 64, inputs), jnp.float32),
        scratch_shapes=[
            pltpu.VMEM((2, 64, inputs), jnp.float32),
            pltpu.SemaphoreType.DMA((inputs // 256,)),
        ],
        name="products",
    )(everyone)


def body(voltages):
    taps = jnp.asarray(make_taps())
    table = jnp.asarray(make_table())
    sent = channelize(voltages, taps, table)
    recv = lax.all_to_all(sent, "y", split_axis=0, concat_axis=0, tiled=True)
    line = add_row(recv)
    recv = lax.all_to_all(line, ("zh", "zl"), split_axis=0, concat_axis=0, tiled=True)
    mine = add_line(recv, 4)
    row = lax.all_to_all(mine, "x", split_axis=0, concat_axis=0, tiled=True)
    row = row.reshape(8, BLOCKS * KEEP, 128)
    everyone = lax.all_gather(row, "c", axis=0)
    return products(everyone)


def solution(mesh):
    fine = Mesh(mesh.devices.reshape(8, 4, 4, 2, 2), ("zl", "y", "x", "zh", "c"))
    return jax.shard_map(
        body,
        mesh=fine,
        in_specs=(P(None, ("x", "zh", "c"), ("zl", "y")),),
        out_specs=P(("zl", "y"), None, ("x", "zh", "c"), None),
        check_vma=False,
    )
```

```python
import jax
import jax.numpy as jnp
import numpy as np
from jax import lax
from jax.experimental import pallas as pl
from jax.experimental.pallas import tpu as pltpu
from jax.sharding import Mesh
from jax.sharding import PartitionSpec as P

F = 4096
TAPS = 16
NS = 113
KEEP = 32
HALF = KEEP // 2
MIDDLE = F // 2
BLOCKS = 4
GROUPS = 5
ROW = 4
LINE = KEEP // ROW
TABLE = 40
SPAN = 32
CUTS = (0, 1024, 2560, 4096)
STEPS = len(CUTS) - 1
FINE = (7, 8)
EDGE = KEEP * TAPS
FINES = EDGE + TAPS
FINE_EDGE = FINES + KEEP * len(FINE)
ROWS = FINE_EDGE + TAPS


def make_taps():
    j = np.arange(TAPS * F, dtype=np.float64)
    total = float(TAPS * F)
    proto = np.sinc((j - total / 2.0 + 0.5) / F) * (
        0.5 - 0.5 * np.cos(2.0 * np.pi * (j + 0.5) / total)
    )
    proto = proto.reshape(TAPS, F)
    taps = proto / np.sqrt(np.sum(proto * proto, axis=0, keepdims=True))
    return taps[::-1].astype(np.float32)


def make_table():
    turns = (MIDDLE + np.arange(HALF + 1))[:, None] * np.arange(F)[None, :] % F
    phase = 2.0 * np.pi * turns / F
    cosine, sine = np.cos(phase) * F**-0.5, np.sin(phase) * F**-0.5
    rows = [cosine[:HALF], cosine[HALF:], sine[1:], np.zeros((TABLE - KEEP - 1, F))]
    table = np.concatenate(rows, axis=0).astype(np.float32)
    return table.astype(jnp.bfloat16).astype(np.float32)


def split(weight):
    high = weight.astype(jnp.bfloat16)
    return high, (weight - high.astype(jnp.float32)).astype(jnp.bfloat16)


def channelize_kernel(x_hbm, table_hbm, out_ref, x, table, acc, parts, sems):
    copies = []
    for j in range(STEPS):
        size = CUTS[j + 1] - CUTS[j]
        here = pl.ds(CUTS[j], size)
        own = [
            pltpu.make_async_copy(table_hbm.at[:, here], table.at[:, here], sems.at[j, 0]),
        ]
        for b in range(BLOCKS):
            at = pl.ds(b * F + CUTS[j], size)
            copy = pltpu.make_async_copy(
                x_hbm.at[:, at], x.at[128 * b : 128 * (b + 1), here], sems.at[j, 1 + b]
            )
            own.append(copy)
        for copy in own:
            copy.start()
        copies.append(own)

    for j in range(STEPS):
        here = slice(CUTS[j], CUTS[j + 1])
        for copy in copies[j][:1]:
            copy.wait()
        tap = table[:TAPS, here]
        wide = table[TAPS:, here]
        main, fine = [], []
        for i in range(TAPS):
            high, low = split(wide[:KEEP] * tap[i : i + 1])
            main.append(high)
            if i in FINE:
                fine.append(low)
        high, low = split(tap * wide[KEEP : KEEP + 1])
        weights = jnp.concatenate(main + [high] + fine + [low], axis=0)
        for copy in copies[j][1:]:
            copy.wait()
        product = lax.dot_general(
            weights, x[:, here], (((1,), (1,)), ((), ())), preferred_element_type=jnp.float32
        )
        if j == 0:
            acc[...] = product
        else:
            acc[...] += product

    lane = lax.broadcasted_iota(jnp.int32, (1, 128), 1)
    sign = jnp.where(lane < 64, 1.0, -1.0).astype(jnp.float32)
    row = lax.broadcasted_iota(jnp.int32, (HALF, 128), 0)
    for m in range(GROUPS * BLOCKS):
        cosine = jnp.zeros((HALF, 128), jnp.float32)
        sine = jnp.zeros((HALF, 128), jnp.float32)
        for b in range(BLOCKS):
            i = m - b
            if not 0 <= i < TAPS:
                continue
            rows = [KEEP * i]
            if i in FINE:
                rows.append(FINES + KEEP * FINE.index(i))
            for at in rows:
                cosine += acc[at : at + HALF, 128 * b : 128 * (b + 1)]
                sine += acc[at + HALF : at + KEEP, 128 * b : 128 * (b + 1)]
        turned = jnp.where(row == 0, 0.0, sign * pltpu.roll(sine, 64, 1))
        parts[KEEP * m : KEEP * m + HALF, :] = cosine + turned
        parts[KEEP * m + HALF : KEEP * (m + 1), :] = jnp.where(row == 0, sine, cosine - turned)

    def put(channel, group, rows):
        out_ref[channel % ROW, channel // ROW, group] = rows.astype(jnp.bfloat16)

    edge = acc[EDGE:FINES, :] + acc[FINE_EDGE:ROWS, :]
    total = jnp.zeros((GROUPS * BLOCKS, 128), jnp.float32)
    for b in range(BLOCKS):
        pieces = [edge[:, 128 * b : 128 * (b + 1)], jnp.zeros((BLOCKS - b, 128), jnp.float32)]
        if b:
            pieces.insert(0, jnp.zeros((b, 128), jnp.float32))
        total += jnp.concatenate(pieces, axis=0)
    total = sign * pltpu.roll(total, 64, 1)
    for p in range(HALF):
        for a in range(GROUPS):
            above = parts[pl.ds(KEEP * BLOCKS * a + p, BLOCKS, stride=KEEP), :]
            put(HALF + p, a, above)
            below = parts[pl.ds(KEEP * BLOCKS * a + HALF + p, BLOCKS, stride=KEEP), :]
            if p:
                put(HALF - p, a, below)
            else:
                put(0, a, below - total[BLOCKS * a : BLOCKS * (a + 1)])


def channelize(voltages, table):
    samples = voltages.reshape(128, BLOCKS * F)
    samples, table = (
        pltpu.with_memory_space_constraint(array, pltpu.HBM) for array in (samples, table)
    )
    anywhere = pl.BlockSpec(memory_space=pltpu.HBM)
    return pl.pallas_call(
        channelize_kernel,
        in_specs=[anywhere] * 2,
        out_specs=pl.BlockSpec(memory_space=pltpu.VMEM),
        out_shape=pltpu.VMEM((ROW, LINE, GROUPS, BLOCKS, 128), jnp.bfloat16),
        scratch_shapes=[
            pltpu.VMEM((128 * BLOCKS, F), jnp.bfloat16),
            pltpu.VMEM((TAPS + TABLE, F), jnp.float32),
            pltpu.VMEM((ROWS, BLOCKS * 128), jnp.float32),
            pltpu.VMEM((GROUPS * BLOCKS * KEEP, 128), jnp.float32),
            pltpu.SemaphoreType.DMA((STEPS, 1 + BLOCKS)),
        ],
        compiler_params=pltpu.CompilerParams(vmem_limit_bytes=40 * 1024 * 1024),
        name="channelize",
    )(samples, table)


def row_kernel(recv_ref, out_ref, wide):
    for g in range(SPAN // BLOCKS):
        total = None
        for y in range(ROW):
            if 0 <= g - y < GROUPS:
                share = recv_ref[y, :, g - y].astype(jnp.float32)
                total = share if total is None else total + share
        wide[:, BLOCKS * g : BLOCKS * (g + 1), :] = total
    done = wide[...].astype(jnp.bfloat16)
    out_ref[:LINE] = done
    out_ref[LINE:] = done


def add_row(recv):
    recv = pltpu.with_memory_space_constraint(recv, pltpu.VMEM)
    return pl.pallas_call(
        row_kernel,
        in_specs=[pl.BlockSpec(memory_space=pltpu.VMEM)],
        out_specs=pl.BlockSpec(memory_space=pltpu.VMEM),
        out_shape=pltpu.VMEM((2 * LINE, SPAN, 128), jnp.bfloat16),
        scratch_shapes=[pltpu.VMEM((LINE, SPAN, 128), jnp.float32)],
        name="add_row",
    )(recv)


def line_kernel(recv_ref, out_ref):
    for z in range(2):
        for d in range(LINE):
            total = recv_ref[LINE * z + d, :TAPS].astype(jnp.float32)
            if d:
                total += recv_ref[LINE * z + d - 1, TAPS:].astype(jnp.float32)
            else:
                row = lax.broadcasted_iota(jnp.int32, total.shape, 0)
                total = jnp.where(row == TAPS - 1, total, 0.0)
            done = total.astype(jnp.bfloat16)
            for x in range(out_ref.shape[0]):
                out_ref[x, z, TAPS * d : TAPS * (d + 1), :] = done


def add_line(recv, copies):
    recv = pltpu.with_memory_space_constraint(recv, pltpu.VMEM)
    return pl.pallas_call(
        line_kernel,
        in_specs=[pl.BlockSpec(memory_space=pltpu.VMEM)],
        out_specs=pl.BlockSpec(memory_space=pltpu.VMEM),
        out_shape=pltpu.VMEM((copies, 2, BLOCKS * KEEP, 128), jnp.bfloat16),
        name="add_line",
    )(recv)


def products_kernel(all_ref, out_hbm, done, sems):
    own = 2 * lax.axis_index("x") + lax.axis_index("zh")
    mine = all_ref[lax.axis_index("c"), own].astype(jnp.float32)
    lane = lax.broadcasted_iota(jnp.int32, mine.shape, 1)
    first = lane < 64
    turned = pltpu.roll(mine, 64, 1) * jnp.where(first, 1.0, -1.0)
    left = jnp.concatenate([mine.T, turned.T], axis=1).astype(jnp.bfloat16)
    copies = []
    for x in range(all_ref.shape[1] // 2):
        real, imag = [], []
        for pair in (2 * x, 2 * x + 1):
            one = all_ref[0, pair].astype(jnp.float32)
            two = all_ref[1, pair].astype(jnp.float32)
            real.append(jnp.where(first, one, pltpu.roll(two, 64, 1)))
            imag.append(jnp.where(first, pltpu.roll(one, 64, 1), two))
        right = jnp.concatenate(
            [jnp.concatenate(real, axis=1), jnp.concatenate(imag, axis=1)], axis=0
        ).astype(jnp.bfloat16)
        full = jnp.dot(left, right, preferred_element_type=jnp.float32) * (1.0 / NS)
        here = slice(256 * x, 256 * (x + 1))
        done[0, :, here] = full[:64]
        done[1, :, here] = full[64:]
        at = pl.ds(256 * x, 256)
        copy = pltpu.make_async_copy(done.at[:, :, at], out_hbm.at[0, :, :, at], sems.at[x])
        copy.start()
        copies.append(copy)
    for copy in copies:
        copy.wait()


def products(everyone):
    inputs = 128 * everyone.shape[1]
    everyone = pltpu.with_memory_space_constraint(everyone, pltpu.VMEM)
    return pl.pallas_call(
        products_kernel,
        in_specs=[pl.BlockSpec(memory_space=pltpu.VMEM)],
        out_specs=pl.BlockSpec(memory_space=pltpu.HBM),
        out_shape=jax.ShapeDtypeStruct((1, 2, 64, inputs), jnp.float32),
        scratch_shapes=[
            pltpu.VMEM((2, 64, inputs), jnp.float32),
            pltpu.SemaphoreType.DMA((inputs // 256,)),
        ],
        name="products",
    )(everyone)


def body(voltages):
    table = jnp.asarray(np.concatenate([make_taps(), make_table()], axis=0))
    sent = channelize(voltages, table)
    recv = lax.all_to_all(sent, "y", split_axis=0, concat_axis=0, tiled=True)
    line = add_row(recv)
    recv = lax.all_to_all(line, ("zh", "zl"), split_axis=0, concat_axis=0, tiled=True)
    mine = add_line(recv, 4)
    row = lax.all_to_all(mine, "x", split_axis=0, concat_axis=0, tiled=True)
    row = row.reshape(8, BLOCKS * KEEP, 128)
    everyone = lax.all_gather(row, "c", axis=0)
    return products(everyone)


def solution(mesh):
    fine = Mesh(mesh.devices.reshape(8, 4, 4, 2, 2), ("zl", "y", "x", "zh", "c"))
    return jax.shard_map(
        body,
        mesh=fine,
        in_specs=(P(None, ("x", "zh", "c"), ("zl", "y")),),
        out_specs=P(("zl", "y"), None, ("x", "zh", "c"), None),
        check_vma=False,
    )
```

```python
import jax
import jax.numpy as jnp
import numpy as np
from jax import lax
from jax.experimental import pallas as pl
from jax.experimental.pallas import tpu as pltpu
from jax.sharding import Mesh
from jax.sharding import PartitionSpec as P

F = 4096
TAPS = 16
NS = 113
KEEP = 32
HALF = KEEP // 2
MIDDLE = F // 2
BLOCKS = 4
GROUPS = 5
ROW = 4
LINE = KEEP // ROW
TABLE = 40
SPAN = 32
CUTS = (0, 1024, 2560, 4096)
STEPS = len(CUTS) - 1
FINE = (7, 8)
EDGE = KEEP * TAPS
FINES = EDGE + TAPS
FINE_EDGE = FINES + KEEP * len(FINE)
ROWS = FINE_EDGE + TAPS


def make_taps():
    j = np.arange(TAPS * F, dtype=np.float64)
    total = float(TAPS * F)
    proto = np.sinc((j - total / 2.0 + 0.5) / F) * (
        0.5 - 0.5 * np.cos(2.0 * np.pi * (j + 0.5) / total)
    )
    proto = proto.reshape(TAPS, F)
    taps = proto / np.sqrt(np.sum(proto * proto, axis=0, keepdims=True))
    return taps[::-1].astype(np.float32)


def make_table():
    turns = (MIDDLE + np.arange(HALF + 1))[:, None] * np.arange(F)[None, :] % F
    phase = 2.0 * np.pi * turns / F
    cosine, sine = np.cos(phase) * F**-0.5, np.sin(phase) * F**-0.5
    rows = [cosine[:HALF], cosine[HALF:], sine[1:], np.zeros((TABLE - KEEP - 1, F))]
    table = np.concatenate(rows, axis=0).astype(np.float32)
    return table.astype(jnp.bfloat16).astype(np.float32)


def split(weight):
    high = weight.astype(jnp.bfloat16)
    return high, (weight - high.astype(jnp.float32)).astype(jnp.bfloat16)


def channelize_kernel(x_hbm, table_hbm, out_ref, x, table, acc, parts, sems):
    copies = []
    for j in range(STEPS):
        size = CUTS[j + 1] - CUTS[j]
        here = pl.ds(CUTS[j], size)
        own = [
            pltpu.make_async_copy(table_hbm.at[:, here], table.at[:, here], sems.at[j, 0]),
        ]
        for b in range(BLOCKS):
            at = pl.ds(b * F + CUTS[j], size)
            copy = pltpu.make_async_copy(
                x_hbm.at[:, at], x.at[128 * b : 128 * (b + 1), here], sems.at[j, 1 + b]
            )
            own.append(copy)
        for copy in own:
            copy.start()
        copies.append(own)

    for j in range(STEPS):
        here = slice(CUTS[j], CUTS[j + 1])
        for copy in copies[j][:1]:
            copy.wait()
        tap = table[:TAPS, here]
        wide = table[TAPS:, here]
        main, fine = [], []
        for i in range(TAPS):
            high, low = split(wide[:KEEP] * tap[i : i + 1])
            main.append(high)
            if i in FINE:
                fine.append(low)
        high, low = split(tap * wide[KEEP : KEEP + 1])
        weights = jnp.concatenate(main + [high] + fine + [low], axis=0)
        for copy in copies[j][1:]:
            copy.wait()
        product = lax.dot_general(
            weights, x[:, here], (((1,), (1,)), ((), ())), preferred_element_type=jnp.float32
        )
        if j == 0:
            acc[...] = product
        else:
            acc[...] += product

    lane = lax.broadcasted_iota(jnp.int32, (1, 128), 1)
    sign = jnp.where(lane < 64, 1.0, -1.0).astype(jnp.float32)
    row = lax.broadcasted_iota(jnp.int32, (HALF, 128), 0)
    for m in range(GROUPS * BLOCKS):
        cosine = jnp.zeros((HALF, 128), jnp.float32)
        sine = jnp.zeros((HALF, 128), jnp.float32)
        for b in range(BLOCKS):
            i = m - b
            if not 0 <= i < TAPS:
                continue
            rows = [KEEP * i]
            if i in FINE:
                rows.append(FINES + KEEP * FINE.index(i))
            for at in rows:
                cosine += acc[at : at + HALF, 128 * b : 128 * (b + 1)]
                sine += acc[at + HALF : at + KEEP, 128 * b : 128 * (b + 1)]
        turned = jnp.where(row == 0, 0.0, sign * pltpu.roll(sine, 64, 1))
        parts[KEEP * m : KEEP * m + HALF, :] = cosine + turned
        parts[KEEP * m + HALF : KEEP * (m + 1), :] = jnp.where(row == 0, sine, cosine - turned)

    def put(channel, group, rows):
        out_ref[channel % ROW, channel // ROW, group] = rows.astype(jnp.bfloat16)

    edge = acc[EDGE:FINES, :] + acc[FINE_EDGE:ROWS, :]
    total = jnp.zeros((GROUPS * BLOCKS, 128), jnp.float32)
    for b in range(BLOCKS):
        pieces = [edge[:, 128 * b : 128 * (b + 1)], jnp.zeros((BLOCKS - b, 128), jnp.float32)]
        if b:
            pieces.insert(0, jnp.zeros((b, 128), jnp.float32))
        total += jnp.concatenate(pieces, axis=0)
    total = sign * pltpu.roll(total, 64, 1)
    for p in range(HALF):
        for a in range(GROUPS):
            above = parts[pl.ds(KEEP * BLOCKS * a + p, BLOCKS, stride=KEEP), :]
            put(HALF + p, a, above)
            below = parts[pl.ds(KEEP * BLOCKS * a + HALF + p, BLOCKS, stride=KEEP), :]
            if p:
                put(HALF - p, a, below)
            else:
                put(0, a, below - total[BLOCKS * a : BLOCKS * (a + 1)])


def channelize(voltages, table):
    samples = voltages.reshape(128, BLOCKS * F)
    samples, table = (
        pltpu.with_memory_space_constraint(array, pltpu.HBM) for array in (samples, table)
    )
    anywhere = pl.BlockSpec(memory_space=pltpu.HBM)
    return pl.pallas_call(
        channelize_kernel,
        in_specs=[anywhere] * 2,
        out_specs=pl.BlockSpec(memory_space=pltpu.VMEM),
        out_shape=pltpu.VMEM((ROW, LINE, GROUPS, BLOCKS, 128), jnp.bfloat16),
        scratch_shapes=[
            pltpu.VMEM((128 * BLOCKS, F), jnp.bfloat16),
            pltpu.VMEM((TAPS + TABLE, F), jnp.float32),
            pltpu.VMEM((ROWS, BLOCKS * 128), jnp.float32),
            pltpu.VMEM((GROUPS * BLOCKS * KEEP, 128), jnp.float32),
            pltpu.SemaphoreType.DMA((STEPS, 1 + BLOCKS)),
        ],
        compiler_params=pltpu.CompilerParams(vmem_limit_bytes=40 * 1024 * 1024),
        name="channelize",
    )(samples, table)


def row_kernel(recv_ref, out_ref, wide):
    for g in range(SPAN // BLOCKS):
        total = None
        for y in range(ROW):
            if 0 <= g - y < GROUPS:
                share = recv_ref[y, :, g - y].astype(jnp.float32)
                total = share if total is None else total + share
        wide[:, BLOCKS * g : BLOCKS * (g + 1), :] = total
    done = wide[...].astype(jnp.bfloat16)
    out_ref[:LINE] = done
    out_ref[LINE:] = done


def add_row(recv):
    recv = pltpu.with_memory_space_constraint(recv, pltpu.VMEM)
    return pl.pallas_call(
        row_kernel,
        in_specs=[pl.BlockSpec(memory_space=pltpu.VMEM)],
        out_specs=pl.BlockSpec(memory_space=pltpu.VMEM),
        out_shape=pltpu.VMEM((2 * LINE, SPAN, 128), jnp.bfloat16),
        scratch_shapes=[pltpu.VMEM((LINE, SPAN, 128), jnp.float32)],
        name="add_row",
    )(recv)


def line_kernel(recv_ref, out_ref):
    for z in range(2):
        for d in range(LINE):
            total = recv_ref[LINE * z + d, :TAPS].astype(jnp.float32)
            if d:
                total += recv_ref[LINE * z + d - 1, TAPS:].astype(jnp.float32)
            else:
                row = lax.broadcasted_iota(jnp.int32, total.shape, 0)
                total = jnp.where(row == TAPS - 1, total, 0.0)
            done = total.astype(jnp.bfloat16)
            for x in range(out_ref.shape[0]):
                out_ref[x, z, TAPS * d : TAPS * (d + 1), :] = done


def add_line(recv, copies):
    recv = pltpu.with_memory_space_constraint(recv, pltpu.VMEM)
    return pl.pallas_call(
        line_kernel,
        in_specs=[pl.BlockSpec(memory_space=pltpu.VMEM)],
        out_specs=pl.BlockSpec(memory_space=pltpu.VMEM),
        out_shape=pltpu.VMEM((copies, 2, BLOCKS * KEEP, 128), jnp.bfloat16),
        name="add_line",
    )(recv)


def products_kernel(all_ref, out_hbm, done, sems):
    own = 2 * lax.axis_index("x") + lax.axis_index("zh")
    turn = (lax.axis_index("x") // 2 + lax.axis_index("zh")) % 2
    mine = all_ref[lax.axis_index("c"), own].astype(jnp.float32)
    lane = lax.broadcasted_iota(jnp.int32, mine.shape, 1)
    first = lane < 64
    turned = pltpu.roll(mine, 64, 1) * jnp.where(first, 1.0, -1.0)
    left = jnp.concatenate([mine.T, turned.T], axis=1).astype(jnp.bfloat16)
    copies = []
    for x in range(all_ref.shape[1] // 2):
        real, imag = [], []
        for pair in (2 * x, 2 * x + 1):
            core = turn if (x // 2 + pair) % 2 == 0 else 1 - turn
            one = all_ref[core, pair].astype(jnp.float32)
            two = all_ref[1 - core, pair].astype(jnp.float32)
            real.append(jnp.where(first, one, pltpu.roll(two, 64, 1)))
            imag.append(jnp.where(first, pltpu.roll(one, 64, 1), two))
        right = jnp.concatenate(
            [jnp.concatenate(real, axis=1), jnp.concatenate(imag, axis=1)], axis=0
        ).astype(jnp.bfloat16)
        full = jnp.dot(left, right, preferred_element_type=jnp.float32) * (1.0 / NS)
        here = slice(256 * x, 256 * (x + 1))
        done[0, :, here] = full[:64]
        done[1, :, here] = full[64:]
        at = pl.ds(256 * x, 256)
        copy = pltpu.make_async_copy(done.at[:, :, at], out_hbm.at[0, :, :, at], sems.at[x])
        copy.start()
        copies.append(copy)
    for copy in copies:
        copy.wait()


def products(everyone):
    inputs = 128 * everyone.shape[1]
    everyone = pltpu.with_memory_space_constraint(everyone, pltpu.VMEM)
    return pl.pallas_call(
        products_kernel,
        in_specs=[pl.BlockSpec(memory_space=pltpu.VMEM)],
        out_specs=pl.BlockSpec(memory_space=pltpu.HBM),
        out_shape=jax.ShapeDtypeStruct((1, 2, 64, inputs), jnp.float32),
        scratch_shapes=[
            pltpu.VMEM((2, 64, inputs), jnp.float32),
            pltpu.SemaphoreType.DMA((inputs // 256,)),
        ],
        name="products",
    )(everyone)


def body(voltages):
    table = jnp.asarray(np.concatenate([make_taps(), make_table()], axis=0))
    sent = channelize(voltages, table)
    recv = lax.all_to_all(sent, "y", split_axis=0, concat_axis=0, tiled=True)
    line = add_row(recv)
    groups = [[2 * z + (core ^ z // LINE) for z in range(2 * LINE)] for core in range(2)]
    recv = lax.all_to_all(
        line, ("zh", "zl", "c"), split_axis=0, concat_axis=0, axis_index_groups=groups, tiled=True
    )
    mine = add_line(recv, 4)
    groups = [[2 * x + (core ^ x // 2) for x in range(4)] for core in range(2)]
    row = lax.all_to_all(
        mine, ("x", "c"), split_axis=0, concat_axis=0, axis_index_groups=groups, tiled=True
    )
    row = row.reshape(8, BLOCKS * KEEP, 128)
    everyone = lax.all_gather(row, "c", axis=0)
    return products(everyone)


def solution(mesh):
    fine = Mesh(mesh.devices.reshape(8, 4, 4, 2, 2), ("zl", "y", "x", "zh", "c"))
    return jax.shard_map(
        body,
        mesh=fine,
        in_specs=(P(None, ("x", "zh", "c"), ("zl", "y")),),
        out_specs=P(("zl", "y"), None, ("x", "zh", "c"), None),
        check_vma=False,
    )
```

```python
import jax
import jax.numpy as jnp
import numpy as np
from jax import lax
from jax.experimental import pallas as pl
from jax.experimental.pallas import tpu as pltpu
from jax.sharding import Mesh
from jax.sharding import PartitionSpec as P

F = 4096
TAPS = 16
NS = 113
KEEP = 32
HALF = KEEP // 2
MIDDLE = F // 2
BLOCKS = 4
GROUPS = 5
ROW = 4
LINE = KEEP // ROW
TABLE = 40
Z_ORDER = tuple(5 * at % 16 for at in range(16))
RING = (0, 2, 1, 3)
SPAN = 32
CUTS = (0, 1024, 2560, 4096)
STEPS = len(CUTS) - 1
FINE = (7, 8)
EDGE = KEEP * TAPS
FINES = EDGE + TAPS
FINE_EDGE = FINES + KEEP * len(FINE)
ROWS = FINE_EDGE + TAPS


def make_taps():
    j = np.arange(TAPS * F, dtype=np.float64)
    total = float(TAPS * F)
    proto = np.sinc((j - total / 2.0 + 0.5) / F) * (
        0.5 - 0.5 * np.cos(2.0 * np.pi * (j + 0.5) / total)
    )
    proto = proto.reshape(TAPS, F)
    taps = proto / np.sqrt(np.sum(proto * proto, axis=0, keepdims=True))
    return taps[::-1].astype(np.float32)


def make_table():
    turns = (MIDDLE + np.arange(HALF + 1))[:, None] * np.arange(F)[None, :] % F
    phase = 2.0 * np.pi * turns / F
    cosine, sine = np.cos(phase) * F**-0.5, np.sin(phase) * F**-0.5
    rows = [cosine[:HALF], cosine[HALF:], sine[1:], np.zeros((TABLE - KEEP - 1, F))]
    table = np.concatenate(rows, axis=0).astype(np.float32)
    return table.astype(jnp.bfloat16).astype(np.float32)


def split(weight):
    high = weight.astype(jnp.bfloat16)
    return high, (weight - high.astype(jnp.float32)).astype(jnp.bfloat16)


def channelize_kernel(x_hbm, table_hbm, out_ref, x, table, acc, parts, sems):
    copies = []
    for j in range(STEPS):
        size = CUTS[j + 1] - CUTS[j]
        here = pl.ds(CUTS[j], size)
        own = [
            pltpu.make_async_copy(table_hbm.at[:, here], table.at[:, here], sems.at[j, 0]),
        ]
        for b in range(BLOCKS):
            at = pl.ds(b * F + CUTS[j], size)
            copy = pltpu.make_async_copy(
                x_hbm.at[:, at], x.at[128 * b : 128 * (b + 1), here], sems.at[j, 1 + b]
            )
            own.append(copy)
        for copy in own:
            copy.start()
        copies.append(own)

    for j in range(STEPS):
        here = slice(CUTS[j], CUTS[j + 1])
        for copy in copies[j][:1]:
            copy.wait()
        tap = table[:TAPS, here]
        wide = table[TAPS:, here]
        main, fine = [], []
        for i in range(TAPS):
            high, low = split(wide[:KEEP] * tap[i : i + 1])
            main.append(high)
            if i in FINE:
                fine.append(low)
        high, low = split(tap * wide[KEEP : KEEP + 1])
        weights = jnp.concatenate(main + [high] + fine + [low], axis=0)
        for copy in copies[j][1:]:
            copy.wait()
        product = lax.dot_general(
            weights, x[:, here], (((1,), (1,)), ((), ())), preferred_element_type=jnp.float32
        )
        if j == 0:
            acc[...] = product
        else:
            acc[...] += product

    lane = lax.broadcasted_iota(jnp.int32, (1, 128), 1)
    sign = jnp.where(lane < 64, 1.0, -1.0).astype(jnp.float32)
    row = lax.broadcasted_iota(jnp.int32, (HALF, 128), 0)
    for m in range(GROUPS * BLOCKS):
        cosine = jnp.zeros((HALF, 128), jnp.float32)
        sine = jnp.zeros((HALF, 128), jnp.float32)
        for b in range(BLOCKS):
            i = m - b
            if not 0 <= i < TAPS:
                continue
            rows = [KEEP * i]
            if i in FINE:
                rows.append(FINES + KEEP * FINE.index(i))
            for at in rows:
                cosine += acc[at : at + HALF, 128 * b : 128 * (b + 1)]
                sine += acc[at + HALF : at + KEEP, 128 * b : 128 * (b + 1)]
        turned = jnp.where(row == 0, 0.0, sign * pltpu.roll(sine, 64, 1))
        parts[KEEP * m : KEEP * m + HALF, :] = cosine + turned
        parts[KEEP * m + HALF : KEEP * (m + 1), :] = jnp.where(row == 0, sine, cosine - turned)

    def put(channel, group, rows):
        out_ref[channel % ROW, channel // ROW, group] = rows.astype(jnp.bfloat16)

    edge = acc[EDGE:FINES, :] + acc[FINE_EDGE:ROWS, :]
    total = jnp.zeros((GROUPS * BLOCKS, 128), jnp.float32)
    for b in range(BLOCKS):
        pieces = [edge[:, 128 * b : 128 * (b + 1)], jnp.zeros((BLOCKS - b, 128), jnp.float32)]
        if b:
            pieces.insert(0, jnp.zeros((b, 128), jnp.float32))
        total += jnp.concatenate(pieces, axis=0)
    total = sign * pltpu.roll(total, 64, 1)
    for p in range(HALF):
        for a in range(GROUPS):
            above = parts[pl.ds(KEEP * BLOCKS * a + p, BLOCKS, stride=KEEP), :]
            put(HALF + p, a, above)
            below = parts[pl.ds(KEEP * BLOCKS * a + HALF + p, BLOCKS, stride=KEEP), :]
            if p:
                put(HALF - p, a, below)
            else:
                put(0, a, below - total[BLOCKS * a : BLOCKS * (a + 1)])


def channelize(voltages, table):
    samples = voltages.reshape(128, BLOCKS * F)
    samples, table = (
        pltpu.with_memory_space_constraint(array, pltpu.HBM) for array in (samples, table)
    )
    anywhere = pl.BlockSpec(memory_space=pltpu.HBM)
    return pl.pallas_call(
        channelize_kernel,
        in_specs=[anywhere] * 2,
        out_specs=pl.BlockSpec(memory_space=pltpu.VMEM),
        out_shape=pltpu.VMEM((ROW, LINE, GROUPS, BLOCKS, 128), jnp.bfloat16),
        scratch_shapes=[
            pltpu.VMEM((128 * BLOCKS, F), jnp.bfloat16),
            pltpu.VMEM((TAPS + TABLE, F), jnp.float32),
            pltpu.VMEM((ROWS, BLOCKS * 128), jnp.float32),
            pltpu.VMEM((GROUPS * BLOCKS * KEEP, 128), jnp.float32),
            pltpu.SemaphoreType.DMA((STEPS, 1 + BLOCKS)),
        ],
        compiler_params=pltpu.CompilerParams(vmem_limit_bytes=40 * 1024 * 1024),
        name="channelize",
    )(samples, table)


def row_kernel(recv_ref, out_ref, wide):
    for g in range(SPAN // BLOCKS):
        total = None
        for y in range(ROW):
            if 0 <= g - y < GROUPS:
                share = recv_ref[y, :, g - y].astype(jnp.float32)
                total = share if total is None else total + share
        wide[:, BLOCKS * g : BLOCKS * (g + 1), :] = total
    done = wide[...].astype(jnp.bfloat16)
    for at, z in enumerate(Z_ORDER):
        out_ref[at] = done[z % LINE]


def add_row(recv):
    recv = pltpu.with_memory_space_constraint(recv, pltpu.VMEM)
    return pl.pallas_call(
        row_kernel,
        in_specs=[pl.BlockSpec(memory_space=pltpu.VMEM)],
        out_specs=pl.BlockSpec(memory_space=pltpu.VMEM),
        out_shape=pltpu.VMEM((2 * LINE, SPAN, 128), jnp.bfloat16),
        scratch_shapes=[pltpu.VMEM((LINE, SPAN, 128), jnp.float32)],
        name="add_row",
    )(recv)


def line_kernel(recv_ref, out_ref):
    for z in range(2):
        for d in range(LINE):
            total = recv_ref[Z_ORDER.index(LINE * z + d), :TAPS].astype(jnp.float32)
            if d:
                total += recv_ref[Z_ORDER.index(LINE * z + d - 1), TAPS:].astype(jnp.float32)
            else:
                row = lax.broadcasted_iota(jnp.int32, total.shape, 0)
                total = jnp.where(row == TAPS - 1, total, 0.0)
            done = total.astype(jnp.bfloat16)
            for x in range(out_ref.shape[0]):
                out_ref[x, z, TAPS * d : TAPS * (d + 1), :] = done


def add_line(recv, copies):
    recv = pltpu.with_memory_space_constraint(recv, pltpu.VMEM)
    return pl.pallas_call(
        line_kernel,
        in_specs=[pl.BlockSpec(memory_space=pltpu.VMEM)],
        out_specs=pl.BlockSpec(memory_space=pltpu.VMEM),
        out_shape=pltpu.VMEM((copies, 2, BLOCKS * KEEP, 128), jnp.bfloat16),
        name="add_line",
    )(recv)


def products_kernel(all_ref, out_hbm, done, sems):
    place = lax.axis_index("x")
    place = 2 * (place % 2) + place // 2
    own = 2 * place + lax.axis_index("zh")
    turn = (lax.axis_index("x") // 2 + lax.axis_index("zh")) % 2
    mine = all_ref[lax.axis_index("c"), own].astype(jnp.float32)
    lane = lax.broadcasted_iota(jnp.int32, mine.shape, 1)
    first = lane < 64
    turned = pltpu.roll(mine, 64, 1) * jnp.where(first, 1.0, -1.0)
    left = jnp.concatenate([mine.T, turned.T], axis=1).astype(jnp.bfloat16)
    copies = []
    for x in range(all_ref.shape[1] // 2):
        real, imag = [], []
        for pair in (2 * x, 2 * x + 1):
            came = 2 * RING[x] + pair % 2
            core = turn if (x // 2 + pair) % 2 == 0 else 1 - turn
            one = all_ref[core, came].astype(jnp.float32)
            two = all_ref[1 - core, came].astype(jnp.float32)
            real.append(jnp.where(first, one, pltpu.roll(two, 64, 1)))
            imag.append(jnp.where(first, pltpu.roll(one, 64, 1), two))
        right = jnp.concatenate(
            [jnp.concatenate(real, axis=1), jnp.concatenate(imag, axis=1)], axis=0
        ).astype(jnp.bfloat16)
        full = jnp.dot(left, right, preferred_element_type=jnp.float32) * (1.0 / NS)
        here = slice(256 * x, 256 * (x + 1))
        done[0, :, here] = full[:64]
        done[1, :, here] = full[64:]
        at = pl.ds(256 * x, 256)
        copy = pltpu.make_async_copy(done.at[:, :, at], out_hbm.at[0, :, :, at], sems.at[x])
        copy.start()
        copies.append(copy)
    for copy in copies:
        copy.wait()


def products(everyone):
    inputs = 128 * everyone.shape[1]
    everyone = pltpu.with_memory_space_constraint(everyone, pltpu.VMEM)
    return pl.pallas_call(
        products_kernel,
        in_specs=[pl.BlockSpec(memory_space=pltpu.VMEM)],
        out_specs=pl.BlockSpec(memory_space=pltpu.HBM),
        out_shape=jax.ShapeDtypeStruct((1, 2, 64, inputs), jnp.float32),
        scratch_shapes=[
            pltpu.VMEM((2, 64, inputs), jnp.float32),
            pltpu.SemaphoreType.DMA((inputs // 256,)),
        ],
        name="products",
    )(everyone)


def body(voltages):
    table = jnp.asarray(np.concatenate([make_taps(), make_table()], axis=0))
    sent = channelize(voltages, table)
    recv = lax.all_to_all(sent, "y", split_axis=0, concat_axis=0, tiled=True)
    line = add_row(recv)
    groups = [[2 * z + (core ^ z // LINE) for z in Z_ORDER] for core in range(2)]
    recv = lax.all_to_all(
        line, ("zh", "zl", "c"), split_axis=0, concat_axis=0, axis_index_groups=groups, tiled=True
    )
    mine = add_line(recv, 4)
    groups = [[2 * x + (core ^ x // 2) for x in RING] for core in range(2)]
    row = lax.all_to_all(
        mine, ("x", "c"), split_axis=0, concat_axis=0, axis_index_groups=groups, tiled=True
    )
    row = row.reshape(8, BLOCKS * KEEP, 128)
    everyone = lax.all_gather(row, "c", axis=0)
    return products(everyone)


def solution(mesh):
    fine = Mesh(mesh.devices.reshape(8, 4, 4, 2, 2), ("zl", "y", "x", "zh", "c"))
    return jax.shard_map(
        body,
        mesh=fine,
        in_specs=(P(None, ("x", "zh", "c"), ("zl", "y")),),
        out_specs=P(("zl", "y"), None, ("x", "zh", "c"), None),
        check_vma=False,
    )
```

```python
import jax
import jax.numpy as jnp
import numpy as np
from jax import lax
from jax.experimental import pallas as pl
from jax.experimental.pallas import tpu as pltpu
from jax.sharding import Mesh
from jax.sharding import PartitionSpec as P

F = 4096
TAPS = 16
NS = 113
KEEP = 32
HALF = KEEP // 2
MIDDLE = F // 2
BLOCKS = 4
GROUPS = 5
ROW = 4
LINE = KEEP // ROW
TABLE = 40
Z_ORDER = tuple(3 * at % 16 for at in range(16))
RING = (0, 2, 1, 3)
SPAN = 32
CUTS = (0, 1024, 2560, 4096)
STEPS = len(CUTS) - 1
FINE = (7, 8)
EDGE = KEEP * TAPS
FINES = EDGE + TAPS
FINE_EDGE = FINES + KEEP * len(FINE)
ROWS = FINE_EDGE + TAPS


def make_taps():
    j = np.arange(TAPS * F, dtype=np.float64)
    total = float(TAPS * F)
    proto = np.sinc((j - total / 2.0 + 0.5) / F) * (
        0.5 - 0.5 * np.cos(2.0 * np.pi * (j + 0.5) / total)
    )
    proto = proto.reshape(TAPS, F)
    taps = proto / np.sqrt(np.sum(proto * proto, axis=0, keepdims=True))
    return taps[::-1].astype(np.float32)


def make_table():
    turns = (MIDDLE + np.arange(HALF + 1))[:, None] * np.arange(F)[None, :] % F
    phase = 2.0 * np.pi * turns / F
    cosine, sine = np.cos(phase) * F**-0.5, np.sin(phase) * F**-0.5
    rows = [cosine[:HALF], cosine[HALF:], sine[1:], np.zeros((TABLE - KEEP - 1, F))]
    table = np.concatenate(rows, axis=0).astype(np.float32)
    return table.astype(jnp.bfloat16).astype(np.float32)


def split(weight):
    high = weight.astype(jnp.bfloat16)
    return high, (weight - high.astype(jnp.float32)).astype(jnp.bfloat16)


def channelize_kernel(x_hbm, table_hbm, out_ref, x, table, acc, parts, sems):
    copies = []
    for j in range(STEPS):
        size = CUTS[j + 1] - CUTS[j]
        here = pl.ds(CUTS[j], size)
        own = [
            pltpu.make_async_copy(table_hbm.at[:, here], table.at[:, here], sems.at[j, 0]),
        ]
        for b in range(BLOCKS):
            at = pl.ds(b * F + CUTS[j], size)
            copy = pltpu.make_async_copy(
                x_hbm.at[:, at], x.at[128 * b : 128 * (b + 1), here], sems.at[j, 1 + b]
            )
            own.append(copy)
        for copy in own:
            copy.start()
        copies.append(own)

    for j in range(STEPS):
        here = slice(CUTS[j], CUTS[j + 1])
        for copy in copies[j][:1]:
            copy.wait()
        tap = table[:TAPS, here]
        wide = table[TAPS:, here]
        main, fine = [], []
        for i in range(TAPS):
            high, low = split(wide[:KEEP] * tap[i : i + 1])
            main.append(high)
            if i in FINE:
                fine.append(low)
        high, low = split(tap * wide[KEEP : KEEP + 1])
        weights = jnp.concatenate(main + [high] + fine + [low], axis=0)
        for copy in copies[j][1:]:
            copy.wait()
        product = lax.dot_general(
            weights, x[:, here], (((1,), (1,)), ((), ())), preferred_element_type=jnp.float32
        )
        if j == 0:
            acc[...] = product
        else:
            acc[...] += product

    lane = lax.broadcasted_iota(jnp.int32, (1, 128), 1)
    sign = jnp.where(lane < 64, 1.0, -1.0).astype(jnp.float32)
    row = lax.broadcasted_iota(jnp.int32, (HALF, 128), 0)
    for m in range(GROUPS * BLOCKS):
        cosine = jnp.zeros((HALF, 128), jnp.float32)
        sine = jnp.zeros((HALF, 128), jnp.float32)
        for b in range(BLOCKS):
            i = m - b
            if not 0 <= i < TAPS:
                continue
            rows = [KEEP * i]
            if i in FINE:
                rows.append(FINES + KEEP * FINE.index(i))
            for at in rows:
                cosine += acc[at : at + HALF, 128 * b : 128 * (b + 1)]
                sine += acc[at + HALF : at + KEEP, 128 * b : 128 * (b + 1)]
        turned = jnp.where(row == 0, 0.0, sign * pltpu.roll(sine, 64, 1))
        parts[KEEP * m : KEEP * m + HALF, :] = cosine + turned
        parts[KEEP * m + HALF : KEEP * (m + 1), :] = jnp.where(row == 0, sine, cosine - turned)

    def put(channel, group, rows):
        out_ref[RING[channel % ROW], channel // ROW, group] = rows.astype(jnp.bfloat16)

    edge = acc[EDGE:FINES, :] + acc[FINE_EDGE:ROWS, :]
    total = jnp.zeros((GROUPS * BLOCKS, 128), jnp.float32)
    for b in range(BLOCKS):
        pieces = [edge[:, 128 * b : 128 * (b + 1)], jnp.zeros((BLOCKS - b, 128), jnp.float32)]
        if b:
            pieces.insert(0, jnp.zeros((b, 128), jnp.float32))
        total += jnp.concatenate(pieces, axis=0)
    total = sign * pltpu.roll(total, 64, 1)
    for p in range(HALF):
        for a in range(GROUPS):
            above = parts[pl.ds(KEEP * BLOCKS * a + p, BLOCKS, stride=KEEP), :]
            put(HALF + p, a, above)
            below = parts[pl.ds(KEEP * BLOCKS * a + HALF + p, BLOCKS, stride=KEEP), :]
            if p:
                put(HALF - p, a, below)
            else:
                put(0, a, below - total[BLOCKS * a : BLOCKS * (a + 1)])


def channelize(voltages, table):
    samples = voltages.reshape(128, BLOCKS * F)
    samples, table = (
        pltpu.with_memory_space_constraint(array, pltpu.HBM) for array in (samples, table)
    )
    anywhere = pl.BlockSpec(memory_space=pltpu.HBM)
    return pl.pallas_call(
        channelize_kernel,
        in_specs=[anywhere] * 2,
        out_specs=pl.BlockSpec(memory_space=pltpu.VMEM),
        out_shape=pltpu.VMEM((ROW, LINE, GROUPS, BLOCKS, 128), jnp.bfloat16),
        scratch_shapes=[
            pltpu.VMEM((128 * BLOCKS, F), jnp.bfloat16),
            pltpu.VMEM((TAPS + TABLE, F), jnp.float32),
            pltpu.VMEM((ROWS, BLOCKS * 128), jnp.float32),
            pltpu.VMEM((GROUPS * BLOCKS * KEEP, 128), jnp.float32),
            pltpu.SemaphoreType.DMA((STEPS, 1 + BLOCKS)),
        ],
        compiler_params=pltpu.CompilerParams(vmem_limit_bytes=40 * 1024 * 1024),
        name="channelize",
    )(samples, table)


def row_kernel(recv_ref, out_ref, wide):
    for g in range(SPAN // BLOCKS):
        total = None
        for y in range(ROW):
            if 0 <= g - y < GROUPS:
                share = recv_ref[RING[y], :, g - y].astype(jnp.float32)
                total = share if total is None else total + share
        wide[:, BLOCKS * g : BLOCKS * (g + 1), :] = total
    done = wide[...].astype(jnp.bfloat16)
    for at, z in enumerate(Z_ORDER):
        out_ref[at] = done[z % LINE]


def add_row(recv):
    recv = pltpu.with_memory_space_constraint(recv, pltpu.VMEM)
    return pl.pallas_call(
        row_kernel,
        in_specs=[pl.BlockSpec(memory_space=pltpu.VMEM)],
        out_specs=pl.BlockSpec(memory_space=pltpu.VMEM),
        out_shape=pltpu.VMEM((2 * LINE, SPAN, 128), jnp.bfloat16),
        scratch_shapes=[pltpu.VMEM((LINE, SPAN, 128), jnp.float32)],
        name="add_row",
    )(recv)


def line_kernel(recv_ref, out_ref):
    for z in range(2):
        for d in range(LINE):
            total = recv_ref[Z_ORDER.index(LINE * z + d), :TAPS].astype(jnp.float32)
            if d:
                total += recv_ref[Z_ORDER.index(LINE * z + d - 1), TAPS:].astype(jnp.float32)
            else:
                row = lax.broadcasted_iota(jnp.int32, total.shape, 0)
                total = jnp.where(row == TAPS - 1, total, 0.0)
            done = total.astype(jnp.bfloat16)
            for x in range(out_ref.shape[0]):
                out_ref[x, z, TAPS * d : TAPS * (d + 1), :] = done


def add_line(recv, copies):
    recv = pltpu.with_memory_space_constraint(recv, pltpu.VMEM)
    return pl.pallas_call(
        line_kernel,
        in_specs=[pl.BlockSpec(memory_space=pltpu.VMEM)],
        out_specs=pl.BlockSpec(memory_space=pltpu.VMEM),
        out_shape=pltpu.VMEM((copies, 2, BLOCKS * KEEP, 128), jnp.bfloat16),
        name="add_line",
    )(recv)


def products_kernel(all_ref, out_hbm, done, sems):
    place = lax.axis_index("x")
    place = 2 * (place % 2) + place // 2
    own = 2 * place + lax.axis_index("zh")
    turn = (lax.axis_index("x") // 2 + lax.axis_index("zh")) % 2
    mine = all_ref[lax.axis_index("c"), own].astype(jnp.float32)
    lane = lax.broadcasted_iota(jnp.int32, mine.shape, 1)
    first = lane < 64
    turned = pltpu.roll(mine, 64, 1) * jnp.where(first, 1.0, -1.0)
    left = jnp.concatenate([mine.T, turned.T], axis=1).astype(jnp.bfloat16)
    copies = []
    for x in range(all_ref.shape[1] // 2):
        real, imag = [], []
        for pair in (2 * x, 2 * x + 1):
            came = 2 * RING[x] + pair % 2
            core = turn if (x // 2 + pair) % 2 == 0 else 1 - turn
            one = all_ref[core, came].astype(jnp.float32)
            two = all_ref[1 - core, came].astype(jnp.float32)
            real.append(jnp.where(first, one, pltpu.roll(two, 64, 1)))
            imag.append(jnp.where(first, pltpu.roll(one, 64, 1), two))
        right = jnp.concatenate(
            [jnp.concatenate(real, axis=1), jnp.concatenate(imag, axis=1)], axis=0
        ).astype(jnp.bfloat16)
        full = jnp.dot(left, right, preferred_element_type=jnp.float32) * (1.0 / NS)
        here = slice(256 * x, 256 * (x + 1))
        done[0, :, here] = full[:64]
        done[1, :, here] = full[64:]
        at = pl.ds(256 * x, 256)
        copy = pltpu.make_async_copy(done.at[:, :, at], out_hbm.at[0, :, :, at], sems.at[x])
        copy.start()
        copies.append(copy)
    for copy in copies:
        copy.wait()


def products(everyone):
    inputs = 128 * everyone.shape[1]
    everyone = pltpu.with_memory_space_constraint(everyone, pltpu.VMEM)
    return pl.pallas_call(
        products_kernel,
        in_specs=[pl.BlockSpec(memory_space=pltpu.VMEM)],
        out_specs=pl.BlockSpec(memory_space=pltpu.HBM),
        out_shape=jax.ShapeDtypeStruct((1, 2, 64, inputs), jnp.float32),
        scratch_shapes=[
            pltpu.VMEM((2, 64, inputs), jnp.float32),
            pltpu.SemaphoreType.DMA((inputs // 256,)),
        ],
        name="products",
    )(everyone)


def body(voltages):
    table = jnp.asarray(np.concatenate([make_taps(), make_table()], axis=0))
    sent = channelize(voltages, table)
    recv = lax.all_to_all(
        sent, "y", split_axis=0, concat_axis=0, axis_index_groups=[list(RING)], tiled=True
    )
    line = add_row(recv)
    groups = [[2 * z + (core ^ z // LINE) for z in Z_ORDER] for core in range(2)]
    recv = lax.all_to_all(
        line, ("zh", "zl", "c"), split_axis=0, concat_axis=0, axis_index_groups=groups, tiled=True
    )
    mine = add_line(recv, 4)
    groups = [[2 * x + (core ^ x // 2) for x in RING] for core in range(2)]
    row = lax.all_to_all(
        mine, ("x", "c"), split_axis=0, concat_axis=0, axis_index_groups=groups, tiled=True
    )
    row = row.reshape(8, BLOCKS * KEEP, 128)
    everyone = lax.all_gather(row, "c", axis=0)
    return products(everyone)


def solution(mesh):
    fine = Mesh(mesh.devices.reshape(8, 4, 4, 2, 2), ("zl", "y", "x", "zh", "c"))
    return jax.shard_map(
        body,
        mesh=fine,
        in_specs=(P(None, ("x", "zh", "c"), ("zl", "y")),),
        out_specs=P(("zl", "y"), None, ("x", "zh", "c"), None),
        check_vma=False,
    )
```
